512 devices in a mesh: dp: 512 (over y, x, z, core).
Axes of the slice: x: 4, y: 8, z: 8, core: 2. Of those that a mesh axis runs over, the one named last changes fastest.
Arguments:
- images: bfloat16 [262144, 1024], P('dp'), may hold values from -0.1875 to 0.1875
- texts: bfloat16 [262144, 1024], P('dp'), may hold values from -0.1875 to 0.1875
- logit_scale: float32 [1], replicated, may hold values from 4 to 12
- logit_bias: float32 [1], replicated, may hold values from -6 to -2
Outputs:
- grad_images: bfloat16 [262144, 1024], P('dp')
- grad_texts: bfloat16 [262144, 1024], P('dp')
The draws below stay inside these ranges and needn't reach their ends.
All inputs are finite; a program needn't handle non-finite values.
Results may differ from the reference program's by a relative error of at most 0.0065.
Values may be sent and summed in bfloat16 or wider, within the bound.
A program may use at most 64 MiB of HBM per device.

```python
import jax
import jax.numpy as jnp
from jax import lax

D = 1024
ROWS = 512
TOKENS = 262144
N_DP = 512


def block_levels(own_key, shape, split, smallest, top_value):
    def one(position, shards_of):
        draws = jax.random.uniform(jax.random.fold_in(jax.random.fold_in(own_key, 6), position), (shards_of,), jnp.float32, smallest / len(split), top_value / len(split))
        return jnp.repeat(jnp.exp(draws), shape[position] // shards_of).reshape((-1,) + (1,) * (len(shape) - position - 1))

    factor_of = one(*split[0])
    for cut in split[1:]:
        factor_of = factor_of * one(*cut)
    return factor_of


def bell_draw(rng, dims, scale, limit, pieces=(), kind=jnp.bfloat16):
    factor_of = block_levels(rng, dims, pieces, -0.22, 0.18) if pieces else 1.0
    drawn = jax.random.normal(rng, dims, jnp.float32) * scale * factor_of
    return jnp.minimum(jnp.maximum(drawn, -limit), limit).astype(kind)


def setup_inputs(seed: int = 0) -> dict:
    arg_keys = jax.random.split(jax.random.key(seed), 5)
    return {
        "images": bell_draw(arg_keys[0], (TOKENS, D), (D ** -0.5), 0.1875, ((0, 512),)),
        "texts": bell_draw(arg_keys[1], (TOKENS, D), (D ** -0.5), 0.1875, ((0, 512),)),
        "logit_scale": jnp.clip(jax.random.uniform(arg_keys[2], (1,), jnp.float32, 4.0, 12.0), 4.0, 12.0),
        "logit_bias": jnp.clip(jax.random.uniform(arg_keys[3], (1,), jnp.float32, -6.0, -2.0), -6.0, -2.0),
    }


EPS = 1e-06

def unit_rows(rows):
    wide = rows.astype(jnp.float32)
    inverse = lax.rsqrt(lax.optimization_barrier(jnp.sum(wide * wide, axis=1, keepdims=True)) + EPS)
    unit = wide * inverse
    return (unit, unit.astype(jnp.bfloat16), inverse)

def pair_terms(img_cast, txt_cast, scale, offset, own):
    logits = scale * jnp.dot(img_cast, txt_cast.T, preferred_element_type=jnp.float32) + offset
    if own:
        rows_idx = lax.broadcasted_iota(jnp.int32, logits.shape, 0)
        cols_idx = lax.broadcasted_iota(jnp.int32, logits.shape, 1)
        signs = jnp.where(rows_idx == cols_idx, jnp.float32(1.0), jnp.float32(-1.0))
        slope = -signs * jax.nn.sigmoid(-signs * logits)
    else:
        slope = jax.nn.sigmoid(logits)
    weights = (scale * slope).astype(jnp.bfloat16)
    img_part = jnp.dot(weights, txt_cast, preferred_element_type=jnp.float32)
    txt_part = lax.dot_general(weights, img_cast, (((0,), (0,)), ((), ())), preferred_element_type=jnp.float32)
    return (img_part, txt_part)

def unnormalize(grad, unit, inverse):
    return (inverse * (grad - unit * lax.optimization_barrier(jnp.sum(unit * grad, axis=1, keepdims=True)))).astype(jnp.bfloat16)

def reference(images, texts, logit_scale, logit_bias):
    count = N_DP
    img_unit, img_cast, img_inv = unit_rows(images)
    txt_unit, txt_cast, txt_inv = unit_rows(texts)
    img_blocks = img_cast.reshape(count, ROWS, D)
    txt_blocks = txt_cast.reshape(count, ROWS, D)
    scale = logit_scale[0]
    offset = logit_bias[0]

    def visit(accum, index):
        here = img_blocks[index]
        image_grad = jnp.zeros((ROWS, D), jnp.float32)
        for step in range(3):
            owner = ((index - step) % count).astype(jnp.int32)
            remote = txt_blocks[owner]
            img_part, txt_part = pair_terms(here, remote, scale, offset, step == 0)
            image_grad = image_grad + img_part
            rounded = lax.optimization_barrier(txt_part.astype(jnp.bfloat16)).astype(jnp.float32)
            accum = accum.at[owner].add(rounded)
        return (accum, image_grad)
    accum, image_grads = lax.scan(visit, jnp.zeros((count, ROWS, D), jnp.float32), jnp.arange(count, dtype=jnp.int32))
    grad_images = unnormalize(image_grads.reshape(TOKENS, D), img_unit, img_inv)
    grad_texts = unnormalize(accum.reshape(TOKENS, D), txt_unit, txt_inv)
    return (grad_images, grad_texts)
```

```python
import functools

import jax
import jax.numpy as jnp
from jax import lax
from jax.experimental import pallas as pl
from jax.experimental.pallas import tpu as pltpu
from jax.sharding import PartitionSpec as P

EPS = 1e-06
MESH = pl.DeviceIdType.MESH
TILE = 256
NEAR_ROWS = 128
FAR_ROWS = 64


def kernel(
    n,
    img_ref,
    txt_ref,
    scale_ref,
    bias_ref,
    gi_ref,
    gt_ref,
    u_raw,
    v_raw,
    chip_raw,
    near_raw,
    relay_raw,
    far_raw,
    u_unit,
    v_unit,
    block_unit,
    u_inv,
    v_inv,
    u_grad,
    v_grad,
    u_out,
    v_out,
    load_sem,
    chip_send,
    chip_recv,
    near_send,
    near_recv,
    relay_send,
    relay_recv,
    far_send,
    far_recv,
    store_sem,
):
    rows, depth = u_raw.shape
    me = lax.axis_index("dp")
    core = lax.rem(me, 2)
    partner = me + 1 - 2 * core
    near_to = lax.rem(me + 4 * core - 2 + n, n)
    far_to = lax.rem(me + 2 * core - 1 + n, n)
    scale = scale_ref[0]
    bias = bias_ref[0]

    barrier = pltpu.get_barrier_semaphore()
    for by in (-2, -1, 1, 2):
        pl.semaphore_signal(
            barrier, inc=1, device_id=(lax.rem(me + by + n, n),), device_id_type=MESH
        )

    def on_core(which, texts, images):
        @pl.when(core == which)
        def _():
            load_u = pltpu.make_async_copy(texts, u_raw, load_sem.at[0])
            load_v = pltpu.make_async_copy(images, v_raw, load_sem.at[1])
            load_u.start()
            load_v.start()
            pl.semaphore_wait(barrier, 4)
            send_chip(texts).start()
            for k in range(rows // NEAR_ROWS):
                send_near(images, k).start()

    def send_chip(source):
        return pltpu.make_async_remote_copy(
            src_ref=source,
            dst_ref=chip_raw,
            send_sem=chip_send.at[0],
            recv_sem=chip_recv.at[0],
            device_id=(partner,),
            device_id_type=MESH,
        )

    def send_near(source, k):
        part = pl.ds(k * NEAR_ROWS, NEAR_ROWS)
        return pltpu.make_async_remote_copy(
            src_ref=source.at[part],
            dst_ref=near_raw.at[part],
            send_sem=near_send.at[k],
            recv_sem=near_recv.at[k],
            device_id=(near_to,),
            device_id_type=MESH,
        )

    def send_relay(k):
        part = pl.ds(k * NEAR_ROWS, NEAR_ROWS)
        return pltpu.make_async_remote_copy(
            src_ref=near_raw.at[part],
            dst_ref=relay_raw.at[part],
            send_sem=relay_send.at[k],
            recv_sem=relay_recv.at[k],
            device_id=(partner,),
            device_id_type=MESH,
        )

    def send_far(k):
        part = pl.ds(k * FAR_ROWS, FAR_ROWS)
        return pltpu.make_async_remote_copy(
            src_ref=chip_raw.at[part],
            dst_ref=far_raw.at[part],
            send_sem=far_send.at[k],
            recv_sem=far_recv.at[k],
            device_id=(far_to,),
            device_id_type=MESH,
        )

    on_core(0, txt_ref, img_ref)
    on_core(1, img_ref, txt_ref)

    def normalize(raw, unit, start, count, inverses=None):
        for at in range(start, start + count, 64):
            part = pl.ds(at, min(64, count))
            wide = raw[part, :].astype(jnp.float32)
            inverse = lax.rsqrt(jnp.sum(wide * wide, axis=1, keepdims=True) + EPS)
            unit[part, :] = (wide * inverse).astype(jnp.bfloat16)
            if inverses is not None:
                inverses[part, :] = jnp.broadcast_to(inverse, (part.size, inverses.shape[1]))

    def accumulate(own, block, start, count, grad, diagonal=False, first=False):
        part = block[pl.ds(start, count), :]
        for at in range(0, rows, TILE):
            here = pl.ds(at, TILE)
            logits = scale * lax.dot_general(
                own[here, :], part, (((1,), (1,)), ((), ())), preferred_element_type=jnp.float32
            ) + bias
            if diagonal and at == start:
                down = lax.broadcasted_iota(jnp.int32, logits.shape, 0)
                across = lax.broadcasted_iota(jnp.int32, logits.shape, 1)
                signs = jnp.where(down == across, jnp.float32(1.0), jnp.float32(-1.0))
                slope = -signs * jax.nn.sigmoid(-signs * logits)
            else:
                slope = jax.nn.sigmoid(logits)
            weights = (scale * slope).astype(jnp.bfloat16)
            term = jnp.dot(weights, part, preferred_element_type=jnp.float32)
            grad[here, :] = term if first else grad[here, :] + term

    def finish(grad, raw, inverses, out):
        for at in range(0, rows, 64):
            here = pl.ds(at, 64)
            inverse = inverses[here, 0:1]
            wide = grad[here, :]
            unit = raw[here, :].astype(jnp.float32) * inverse
            along = jnp.sum(unit * wide, axis=1, keepdims=True)
            out[here, :] = (inverse * (wide - unit * along)).astype(jnp.bfloat16)

    pltpu.make_async_copy(txt_ref, u_raw, load_sem.at[0]).wait()
    pltpu.make_async_copy(img_ref, v_raw, load_sem.at[1]).wait()
    normalize(u_raw, u_unit, 0, rows, u_inv)
    normalize(v_raw, v_unit, 0, rows, v_inv)
    for start in range(0, rows, TILE):
        accumulate(u_unit, v_unit, start, TILE, u_grad, diagonal=True, first=start == 0)
        accumulate(v_unit, u_unit, start, TILE, v_grad, diagonal=True, first=start == 0)

    send_chip(txt_ref).wait_recv()
    normalize(chip_raw, block_unit, 0, rows)
    for start in range(0, rows, TILE):
        accumulate(u_unit, block_unit, start, TILE, u_grad)

    per_tile = TILE // NEAR_ROWS
    nears = rows // NEAR_ROWS
    fars = rows // FAR_ROWS
    for tile in range(rows // TILE):
        for k in range(tile * per_tile, (tile + 1) * per_tile):
            send_near(img_ref, k).wait_recv()
            send_relay(k).start()
            normalize(near_raw, block_unit, k * NEAR_ROWS, NEAR_ROWS)
        accumulate(u_unit, block_unit, tile * TILE, TILE, u_grad)
    for k in range(nears):
        send_near(img_ref, k).wait_send()
        if k == nears - 2:
            for j in range(2):
                send_far(j).start()
    for tile in range(rows // TILE):
        for k in range(tile * per_tile, (tile + 1) * per_tile):
            send_relay(k).wait_recv()
            normalize(relay_raw, block_unit, k * NEAR_ROWS, NEAR_ROWS)
        accumulate(v_unit, block_unit, tile * TILE, TILE, v_grad)
    finish(u_grad, u_raw, u_inv, u_out)

    def store(source, out, slot):
        return pltpu.make_async_copy(source, out, store_sem.at[slot])

    @pl.when(core == 0)
    def _():
        store(u_out, gt_ref, 0).start()

    @pl.when(core == 1)
    def _():
        store(u_out, gi_ref, 0).start()

    for k in range(fars):
        send_far(k).wait_send()
        if k + 2 < fars:
            send_far(k + 2).start()
        send_far(k).wait_recv()
        normalize(far_raw, block_unit, k * FAR_ROWS, FAR_ROWS)
        accumulate(v_unit, block_unit, k * FAR_ROWS, FAR_ROWS, v_grad)
    finish(v_grad, v_raw, v_inv, v_out)

    @pl.when(core == 0)
    def _():
        store(v_out, gi_ref, 1).start()

    @pl.when(core == 1)
    def _():
        store(v_out, gt_ref, 1).start()

    for k in range(nears):
        send_relay(k).wait_send()
    send_chip(txt_ref).wait_send()
    store(u_out, gt_ref, 0).wait()
    store(v_out, gi_ref, 1).wait()


def solution(mesh):
    n = mesh.shape["dp"]

    def shards(images, texts, logit_scale, logit_bias):
        rows, depth = images.shape
        block = pltpu.VMEM((rows, depth), jnp.bfloat16)
        total = pltpu.VMEM((rows, depth), jnp.float32)
        inverses = pltpu.VMEM((rows, 128), jnp.float32)
        dma = pltpu.SemaphoreType.DMA
        nears, fars = rows // NEAR_ROWS, rows // FAR_ROWS
        result = jax.ShapeDtypeStruct((rows, depth), jnp.bfloat16)
        return pl.pallas_call(
            functools.partial(kernel, n),
            out_shape=(result, result),
            in_specs=[pl.BlockSpec(memory_space=pl.ANY)] * 2
            + [pl.BlockSpec(memory_space=pltpu.SMEM)] * 2,
            out_specs=[pl.BlockSpec(memory_space=pl.ANY)] * 2,
            scratch_shapes=[block] * 6
            + [block] * 3
            + [inverses] * 2
            + [total] * 2
            + [block] * 2
            + [
                dma((2,)),
                dma((1,)),
                dma((1,)),
                dma((nears,)),
                dma((nears,)),
                dma((nears,)),
                dma((nears,)),
                dma((fars,)),
                dma((fars,)),
                dma((2,)),
            ],
            compiler_params=pltpu.CompilerParams(
                collective_id=0, has_side_effects=True, vmem_limit_bytes=48 * 1024 * 1024
            ),
            cost_estimate=pl.CostEstimate(
                flops=24 * rows * rows * depth, bytes_accessed=8 * rows * depth, transcendentals=0
            ),
        )(images, texts, logit_scale, logit_bias)

    in_specs = (P("dp", None), P("dp", None), P(), P())
    out_specs = (P("dp", None), P("dp", None))
    return jax.shard_map(shards, mesh=mesh, in_specs=in_specs, out_specs=out_specs, check_vma=False)
```

```python
import functools

import jax
import jax.numpy as jnp
from jax import lax
from jax.experimental import pallas as pl
from jax.experimental.pallas import tpu as pltpu
from jax.sharding import PartitionSpec as P

EPS = 1e-06
MESH = pl.DeviceIdType.MESH
TILE = 256
NEAR_ROWS = 128
FAR_ROWS = 64
STORE_ROWS = 128


def finish(grad, raw, inverses, out, start, count):
    for at in range(start, start + count, 64):
        here = pl.ds(at, 64)
        inverse = inverses[here, 0:1]
        wide = grad[here, :]
        unit = raw[here, :].astype(jnp.float32) * inverse
        along = jnp.sum(unit * wide, axis=1, keepdims=True)
        out[here, :] = (inverse * (wide - unit * along)).astype(jnp.bfloat16)


def finish_kernel(u_out, v_grad, v_raw, v_inv, gi_ref, gt_ref, v_out, u_sem, v_sem):
    core = lax.rem(lax.axis_index("dp"), 2)
    rows = v_grad.shape[0]

    def store(u_target, v_target):
        pltpu.make_async_copy(u_out, u_target, u_sem).start()
        for slot in range(rows // STORE_ROWS):
            part = pl.ds(slot * STORE_ROWS, STORE_ROWS)
            finish(v_grad, v_raw, v_inv, v_out, slot * STORE_ROWS, STORE_ROWS)
            pltpu.make_async_copy(v_out.at[part], v_target.at[part], v_sem.at[slot]).start()

    @pl.when(core == 0)
    def _():
        store(gt_ref, gi_ref)

    @pl.when(core == 1)
    def _():
        store(gi_ref, gt_ref)

    pltpu.make_async_copy(u_out, gt_ref, u_sem).wait()
    for slot in range(rows // STORE_ROWS):
        part = pl.ds(slot * STORE_ROWS, STORE_ROWS)
        pltpu.make_async_copy(v_out.at[part], gi_ref.at[part], v_sem.at[slot]).wait()


def kernel(
    n,
    img_ref,
    txt_ref,
    scale_ref,
    bias_ref,
    u_out,
    v_grad,
    v_raw,
    v_inv,
    u_raw,
    chip_raw,
    near_raw,
    relay_raw,
    far_raw,
    u_unit,
    v_unit,
    block_unit,
    u_inv,
    u_grad,
    load_sem,
    chip_send,
    chip_recv,
    near_send,
    near_recv,
    relay_send,
    relay_recv,
    far_send,
    far_recv,
):
    rows, depth = u_raw.shape
    me = lax.axis_index("dp")
    core = lax.rem(me, 2)
    partner = me + 1 - 2 * core
    near_to = lax.rem(me + 4 * core - 2 + n, n)
    far_to = lax.rem(me + 2 * core - 1 + n, n)
    scale = scale_ref[0]
    bias = bias_ref[0]

    barrier = pltpu.get_barrier_semaphore()
    near_from = lax.rem(me + 2 - 4 * core + n, n)
    for sender in (partner, near_from, far_to):
        pl.semaphore_signal(barrier, inc=1, device_id=(sender,), device_id_type=MESH)

    def on_core(which, texts, images):
        @pl.when(core == which)
        def _():
            load_u = pltpu.make_async_copy(texts, u_raw, load_sem.at[0])
            load_v = pltpu.make_async_copy(images, v_raw, load_sem.at[1])
            load_u.start()
            load_v.start()
            pl.semaphore_wait(barrier, 3)
            send_chip(texts).start()
            for k in range(rows // NEAR_ROWS):
                send_near(images, k).start()

    def send_chip(source):
        return pltpu.make_async_remote_copy(
            src_ref=source,
            dst_ref=chip_raw,
            send_sem=chip_send.at[0],
            recv_sem=chip_recv.at[0],
            device_id=(partner,),
            device_id_type=MESH,
        )

    def send_near(source, k):
        part = pl.ds(k * NEAR_ROWS, NEAR_ROWS)
        return pltpu.make_async_remote_copy(
            src_ref=source.at[part],
            dst_ref=near_raw.at[part],
            send_sem=near_send.at[k],
            recv_sem=near_recv.at[k],
            device_id=(near_to,),
            device_id_type=MESH,
        )

    def send_relay(k):
        part = pl.ds(k * NEAR_ROWS, NEAR_ROWS)
        return pltpu.make_async_remote_copy(
            src_ref=near_raw.at[part],
            dst_ref=relay_raw.at[part],
            send_sem=relay_send.at[k],
            recv_sem=relay_recv.at[k],
            device_id=(partner,),
            device_id_type=MESH,
        )

    def send_far(k):
        part = pl.ds(k * FAR_ROWS, FAR_ROWS)
        return pltpu.make_async_remote_copy(
            src_ref=chip_raw.at[part],
            dst_ref=far_raw.at[part],
            send_sem=far_send.at[k],
            recv_sem=far_recv.at[k],
            device_id=(far_to,),
            device_id_type=MESH,
        )

    on_core(0, txt_ref, img_ref)
    on_core(1, img_ref, txt_ref)
    send_chip(txt_ref).wait_recv()
    for k in range(rows // FAR_ROWS):
        send_far(k).start()

    def normalize(raw, unit, start, count, inverses=None):
        for at in range(start, start + count, 64):
            part = pl.ds(at, min(64, count))
            wide = raw[part, :].astype(jnp.float32)
            inverse = lax.rsqrt(jnp.sum(wide * wide, axis=1, keepdims=True) + EPS)
            unit[part, :] = (wide * inverse).astype(jnp.bfloat16)
            if inverses is not None:
                inverses[part, :] = jnp.broadcast_to(inverse, (part.size, inverses.shape[1]))

    def accumulate(own, block, start, count, grad, diagonal=False, first=False):
        part = block[pl.ds(start, count), :]
        for at in range(0, rows, TILE):
            here = pl.ds(at, TILE)
            logits = scale * lax.dot_general(
                own[here, :], part, (((1,), (1,)), ((), ())), preferred_element_type=jnp.float32
            ) + bias
            if diagonal and at == start:
                down = lax.broadcasted_iota(jnp.int32, logits.shape, 0)
                across = lax.broadcasted_iota(jnp.int32, logits.shape, 1)
                signs = jnp.where(down == across, jnp.float32(1.0), jnp.float32(-1.0))
                slope = -signs * jax.nn.sigmoid(-signs * logits)
            else:
                slope = jax.nn.sigmoid(logits)
            weights = (scale * slope).astype(jnp.bfloat16)
            term = jnp.dot(weights, part, preferred_element_type=jnp.float32)
            grad[here, :] = term if first else grad[here, :] + term

    pltpu.make_async_copy(txt_ref, u_raw, load_sem.at[0]).wait()
    pltpu.make_async_copy(img_ref, v_raw, load_sem.at[1]).wait()
    normalize(u_raw, u_unit, 0, rows, u_inv)
    normalize(v_raw, v_unit, 0, rows, v_inv)
    for start in range(0, rows, TILE):
        accumulate(u_unit, v_unit, start, TILE, u_grad, diagonal=True, first=start == 0)
        accumulate(v_unit, u_unit, start, TILE, v_grad, diagonal=True, first=start == 0)

    normalize(chip_raw, block_unit, 0, rows)
    for start in range(0, rows, TILE):
        accumulate(u_unit, block_unit, start, TILE, u_grad)

    per_tile = TILE // NEAR_ROWS
    nears = rows // NEAR_ROWS
    fars = rows // FAR_ROWS
    for tile in range(rows // TILE):
        for k in range(tile * per_tile, (tile + 1) * per_tile):
            send_near(img_ref, k).wait_recv()
            send_relay(k).start()
            normalize(near_raw, block_unit, k * NEAR_ROWS, NEAR_ROWS)
        accumulate(u_unit, block_unit, tile * TILE, TILE, u_grad)
    for tile in range(rows // TILE):
        for k in range(tile * per_tile, (tile + 1) * per_tile):
            send_relay(k).wait_recv()
            normalize(relay_raw, block_unit, k * NEAR_ROWS, NEAR_ROWS)
        accumulate(v_unit, block_unit, tile * TILE, TILE, v_grad)
    finish(u_grad, u_raw, u_inv, u_out, 0, rows)

    for k in range(fars):
        send_far(k).wait_recv()
        normalize(far_raw, block_unit, k * FAR_ROWS, FAR_ROWS)
        accumulate(v_unit, block_unit, k * FAR_ROWS, FAR_ROWS, v_grad)

    for k in range(nears):
        send_near(img_ref, k).wait_send()
        send_relay(k).wait_send()
    for k in range(fars):
        send_far(k).wait_send()
    send_chip(txt_ref).wait_send()


def solution(mesh):
    n = mesh.shape["dp"]

    def shards(images, texts, logit_scale, logit_bias):
        rows, depth = images.shape
        block = pltpu.VMEM((rows, depth), jnp.bfloat16)
        total = pltpu.VMEM((rows, depth), jnp.float32)
        inverses = pltpu.VMEM((rows, 128), jnp.float32)
        dma = pltpu.SemaphoreType.DMA
        nears, fars = rows // NEAR_ROWS, rows // FAR_ROWS
        in_vmem = pl.BlockSpec(memory_space=pltpu.VMEM)
        in_hbm = pl.BlockSpec(memory_space=pltpu.HBM)
        images = pltpu.with_memory_space_constraint(images, pltpu.HBM)
        texts = pltpu.with_memory_space_constraint(texts, pltpu.HBM)
        parts = pl.pallas_call(
            functools.partial(kernel, n),
            out_shape=(block, total, block, inverses),
            in_specs=[in_hbm] * 2 + [pl.BlockSpec(memory_space=pltpu.SMEM)] * 2,
            out_specs=[in_vmem] * 4,
            scratch_shapes=[block] * 5
            + [block] * 3
            + [inverses]
            + [total]
            + [
                dma((2,)),
                dma((1,)),
                dma((1,)),
                dma((nears,)),
                dma((nears,)),
                dma((nears,)),
                dma((nears,)),
                dma((fars,)),
                dma((fars,)),
            ],
            compiler_params=pltpu.CompilerParams(
                collective_id=0, has_side_effects=True, vmem_limit_bytes=40 * 1024 * 1024
            ),
            cost_estimate=pl.CostEstimate(
                flops=24 * rows * rows * depth, bytes_accessed=8 * rows * depth, transcendentals=0
            ),
        )(images, texts, logit_scale, logit_bias)
        parts = [pltpu.with_memory_space_constraint(part, pltpu.VMEM) for part in parts]
        result = jax.ShapeDtypeStruct((rows, depth), jnp.bfloat16)
        return pl.pallas_call(
            finish_kernel,
            out_shape=(result, result),
            in_specs=[in_vmem] * 4,
            out_specs=[in_hbm] * 2,
            scratch_shapes=[block, dma, dma((rows // STORE_ROWS,))],
            compiler_params=pltpu.CompilerParams(vmem_limit_bytes=16 * 1024 * 1024),
            cost_estimate=pl.CostEstimate(
                flops=8 * rows * depth, bytes_accessed=4 * rows * depth, transcendentals=0
            ),
        )(*parts)

    in_specs = (P("dp", None), P("dp", None), P(), P())
    out_specs = (P("dp", None), P("dp", None))
    return jax.shard_map(shards, mesh=mesh, in_specs=in_specs, out_specs=out_specs, check_vma=False)
```

```python
import functools

import jax
import jax.numpy as jnp
from jax import lax
from jax.experimental import pallas as pl
from jax.experimental.pallas import tpu as pltpu
from jax.sharding import PartitionSpec as P

EPS = 1e-06
MESH = pl.DeviceIdType.MESH
TILE = 256
NEAR_ROWS = 128
FAR_CHUNKS = ((0, 128), (128, 128), (256, 128), (384, 64), (448, 64))
LAST_ROWS = FAR_CHUNKS[-1][1]
STORE_ROWS = 128


def finish(wide, raw, inverse):
    unit = raw.astype(jnp.float32) * inverse
    along = jnp.sum(unit * wide, axis=1, keepdims=True)
    return (inverse * (wide - unit * along)).astype(jnp.bfloat16)


def finish_kernel(
    u_out, v_grad, v_raw, v_inv, last_unit, last_weights, gi_ref, gt_ref, v_out, u_sem, v_sem
):
    core = lax.rem(lax.axis_index("dp"), 2)
    slots = v_grad.shape[0] // STORE_ROWS

    @pl.when(core == 0)
    def _():
        pltpu.make_async_copy(u_out, gt_ref, u_sem).start()

    @pl.when(core == 1)
    def _():
        pltpu.make_async_copy(u_out, gi_ref, u_sem).start()

    for slot in range(slots):
        part = pl.ds(slot * STORE_ROWS, STORE_ROWS)
        wide = v_grad[part, :] + jnp.dot(
            last_weights[part, :], last_unit[...], preferred_element_type=jnp.float32
        )
        v_out[part, :] = finish(wide, v_raw[part, :], v_inv[part, 0:1])

        @pl.when(core == 0)
        def _():
            pltpu.make_async_copy(v_out.at[part], gi_ref.at[part], v_sem.at[slot]).start()

        @pl.when(core == 1)
        def _():
            pltpu.make_async_copy(v_out.at[part], gt_ref.at[part], v_sem.at[slot]).start()

    pltpu.make_async_copy(u_out, gt_ref, u_sem).wait()
    for slot in range(slots):
        part = pl.ds(slot * STORE_ROWS, STORE_ROWS)
        pltpu.make_async_copy(v_out.at[part], gi_ref.at[part], v_sem.at[slot]).wait()


def kernel(
    n,
    img_ref,
    txt_ref,
    scale_ref,
    bias_ref,
    u_out,
    v_grad,
    v_raw,
    v_inv,
    last_unit,
    last_weights,
    scale_here,
    bias_here,
    u_raw,
    chip_raw,
    near_raw,
    relay_raw,
    far_raw,
    u_unit,
    v_unit,
    block_unit,
    u_inv,
    u_grad,
    load_sem,
    chip_send,
    chip_recv,
    near_send,
    near_recv,
    relay_send,
    relay_recv,
    far_send,
    far_recv,
):
    rows, depth = u_raw.shape
    me = lax.axis_index("dp")
    core = lax.rem(me, 2)
    partner = me + 1 - 2 * core
    near_to = lax.rem(me + 4 * core - 2 + n, n)
    far_to = lax.rem(me + 2 * core - 1 + n, n)

    barrier = pltpu.get_barrier_semaphore()
    near_from = lax.rem(me + 2 - 4 * core + n, n)
    for sender in (partner, near_from, far_to):
        pl.semaphore_signal(barrier, inc=1, device_id=(sender,), device_id_type=MESH)

    load_scale = pltpu.make_async_copy(scale_ref, scale_here, load_sem.at[2])
    load_bias = pltpu.make_async_copy(bias_ref, bias_here, load_sem.at[3])
    load_scale.start()
    load_bias.start()

    def on_core(which, texts, images):
        @pl.when(core == which)
        def _():
            load_u = pltpu.make_async_copy(texts, u_raw, load_sem.at[0])
            load_v = pltpu.make_async_copy(images, v_raw, load_sem.at[1])
            load_u.start()
            load_v.start()
            pl.semaphore_wait(barrier, 3)
            send_chip(texts).start()
            for k in range(rows // NEAR_ROWS):
                send_near(images, k).start()

    def send_chip(source):
        return pltpu.make_async_remote_copy(
            src_ref=source,
            dst_ref=chip_raw,
            send_sem=chip_send.at[0],
            recv_sem=chip_recv.at[0],
            device_id=(partner,),
            device_id_type=MESH,
        )

    def send_near(source, k):
        part = pl.ds(k * NEAR_ROWS, NEAR_ROWS)
        return pltpu.make_async_remote_copy(
            src_ref=source.at[part],
            dst_ref=near_raw.at[part],
            send_sem=near_send.at[k],
            recv_sem=near_recv.at[k],
            device_id=(near_to,),
            device_id_type=MESH,
        )

    def send_relay(k):
        part = pl.ds(k * NEAR_ROWS, NEAR_ROWS)
        return pltpu.make_async_remote_copy(
            src_ref=near_raw.at[part],
            dst_ref=relay_raw.at[part],
            send_sem=relay_send.at[k],
            recv_sem=relay_recv.at[k],
            device_id=(partner,),
            device_id_type=MESH,
        )

    def send_far(k):
        part = pl.ds(*FAR_CHUNKS[k])
        return pltpu.make_async_remote_copy(
            src_ref=chip_raw.at[part],
            dst_ref=far_raw.at[part],
            send_sem=far_send.at[k],
            recv_sem=far_recv.at[k],
            device_id=(far_to,),
            device_id_type=MESH,
        )

    on_core(0, txt_ref, img_ref)
    on_core(1, img_ref, txt_ref)
    send_chip(txt_ref).wait_recv()
    fars = len(FAR_CHUNKS)
    for k in range(fars):
        send_far(k).start()

    def normalize(raw, unit, start, count, inverses=None):
        for at in range(start, start + count, 64):
            part = pl.ds(at, min(64, count))
            wide = raw[part, :].astype(jnp.float32)
            inverse = lax.rsqrt(jnp.sum(wide * wide, axis=1, keepdims=True) + EPS)
            unit[part, :] = (wide * inverse).astype(jnp.bfloat16)
            if inverses is not None:
                inverses[part, :] = jnp.broadcast_to(inverse, (part.size, inverses.shape[1]))

    def weigh(own, part, diagonal=False):
        logits = scale * lax.dot_general(
            own, part, (((1,), (1,)), ((), ())), preferred_element_type=jnp.float32
        ) + bias
        if diagonal:
            down = lax.broadcasted_iota(jnp.int32, logits.shape, 0)
            across = lax.broadcasted_iota(jnp.int32, logits.shape, 1)
            signs = jnp.where(down == across, jnp.float32(1.0), jnp.float32(-1.0))
            slope = -signs * jax.nn.sigmoid(-signs * logits)
        else:
            slope = jax.nn.sigmoid(logits)
        return (scale * slope).astype(jnp.bfloat16)

    def accumulate(own, block, start, count, grad, diagonal=False, first=False):
        part = block[pl.ds(start, count), :]
        for at in range(0, rows, TILE):
            here = pl.ds(at, TILE)
            weights = weigh(own[here, :], part, diagonal and at == start)
            term = jnp.dot(weights, part, preferred_element_type=jnp.float32)
            grad[here, :] = term if first else grad[here, :] + term

    pltpu.make_async_copy(txt_ref, u_raw, load_sem.at[0]).wait()
    pltpu.make_async_copy(img_ref, v_raw, load_sem.at[1]).wait()
    normalize(u_raw, u_unit, 0, rows, u_inv)
    normalize(v_raw, v_unit, 0, rows, v_inv)
    load_scale.wait()
    load_bias.wait()
    scale = scale_here[0]
    bias = bias_here[0]
    for start in range(0, rows, TILE):
        accumulate(u_unit, v_unit, start, TILE, u_grad, diagonal=True, first=start == 0)
        accumulate(v_unit, u_unit, start, TILE, v_grad, diagonal=True, first=start == 0)

    normalize(chip_raw, block_unit, 0, rows)
    for start in range(0, rows, TILE):
        accumulate(u_unit, block_unit, start, TILE, u_grad)

    per_tile = TILE // NEAR_ROWS
    nears = rows // NEAR_ROWS
    for tile in range(rows // TILE):
        for k in range(tile * per_tile, (tile + 1) * per_tile):
            send_near(img_ref, k).wait_recv()
            send_relay(k).start()
            normalize(near_raw, block_unit, k * NEAR_ROWS, NEAR_ROWS)
        accumulate(u_unit, block_unit, tile * TILE, TILE, u_grad)
    for tile in range(rows // TILE):
        for k in range(tile * per_tile, (tile + 1) * per_tile):
            send_relay(k).wait_recv()
            normalize(relay_raw, block_unit, k * NEAR_ROWS, NEAR_ROWS)
        accumulate(v_unit, block_unit, tile * TILE, TILE, v_grad)
    for at in range(0, rows, 64):
        here = pl.ds(at, 64)
        u_out[here, :] = finish(u_grad[here, :], u_raw[here, :], u_inv[here, 0:1])

    for k in range(fars):
        send_far(k).wait_recv()
        start, count = FAR_CHUNKS[k]
        normalize(far_raw, block_unit, start, count)
        if k + 1 < fars:
            accumulate(v_unit, block_unit, start, count, v_grad)
        else:
            last_unit[...] = block_unit[pl.ds(start, count), :]
            for at in range(0, rows, TILE):
                here = pl.ds(at, TILE)
                last_weights[here, :] = weigh(v_unit[here, :], last_unit[...])

    for k in range(nears):
        send_near(img_ref, k).wait_send()
        send_relay(k).wait_send()
    for k in range(fars):
        send_far(k).wait_send()
    send_chip(txt_ref).wait_send()


def solution(mesh):
    n = mesh.shape["dp"]

    def shards(images, texts, logit_scale, logit_bias):
        rows, depth = images.shape
        block = pltpu.VMEM((rows, depth), jnp.bfloat16)
        total = pltpu.VMEM((rows, depth), jnp.float32)
        inverses = pltpu.VMEM((rows, 128), jnp.float32)
        dma = pltpu.SemaphoreType.DMA
        nears, fars = rows // NEAR_ROWS, len(FAR_CHUNKS)
        scalar = pltpu.SMEM((1,), jnp.float32)
        last = pltpu.VMEM((LAST_ROWS, depth), jnp.bfloat16)
        last_weights = pltpu.VMEM((rows, LAST_ROWS), jnp.bfloat16)
        in_vmem = pl.BlockSpec(memory_space=pltpu.VMEM)
        in_hbm = pl.BlockSpec(memory_space=pltpu.HBM)
        operands = [
            pltpu.with_memory_space_constraint(operand, pltpu.HBM)
            for operand in (images, texts)
        ]
        parts = pl.pallas_call(
            functools.partial(kernel, n),
            out_shape=(block, total, block, inverses, last, last_weights),
            in_specs=[in_hbm] * 2 + [pl.BlockSpec(memory_space=pl.ANY)] * 2,
            out_specs=[in_vmem] * 6,
            scratch_shapes=[scalar] * 2
            + [block] * 5
            + [block] * 3
            + [inverses]
            + [total]
            + [
                dma((4,)),
                dma((1,)),
                dma((1,)),
                dma((nears,)),
                dma((nears,)),
                dma((nears,)),
                dma((nears,)),
                dma((fars,)),
                dma((fars,)),
            ],
            compiler_params=pltpu.CompilerParams(
                collective_id=0, has_side_effects=True, vmem_limit_bytes=40 * 1024 * 1024
            ),
            cost_estimate=pl.CostEstimate(
                flops=24 * rows * rows * depth, bytes_accessed=8 * rows * depth, transcendentals=0
            ),
        )(*operands, logit_scale, logit_bias)
        parts = [pltpu.with_memory_space_constraint(part, pltpu.VMEM) for part in parts]
        result = jax.ShapeDtypeStruct((rows, depth), jnp.bfloat16)
        return pl.pallas_call(
            finish_kernel,
            out_shape=(result, result),
            in_specs=[in_vmem] * 6,
            out_specs=[in_hbm] * 2,
            scratch_shapes=[block, dma, dma((rows // STORE_ROWS,))],
            compiler_params=pltpu.CompilerParams(vmem_limit_bytes=16 * 1024 * 1024),
            cost_estimate=pl.CostEstimate(
                flops=8 * rows * depth, bytes_accessed=4 * rows * depth, transcendentals=0
            ),
        )(*parts)

    in_specs = (P("dp", None), P("dp", None), P(), P())
    out_specs = (P("dp", None), P("dp", None))
    return jax.shard_map(shards, mesh=mesh, in_specs=in_specs, out_specs=out_specs, check_vma=False)
```

```python
import functools

import jax
import jax.numpy as jnp
from jax import lax
from jax.experimental import pallas as pl
from jax.experimental.pallas import tpu as pltpu
from jax.sharding import PartitionSpec as P

EPS = 1e-06
MESH = pl.DeviceIdType.MESH
TILE = 256
NEAR_ROWS = 128
FAR_CHUNKS = ((0, 128), (128, 128), (256, 64), (320, 64), (384, 64), (448, 64))
FAR_GROUPS = ((0,), (1,), (2, 3, 4), (5,))
LAST_ROWS = FAR_CHUNKS[-1][1]
LINE = 8
HOP = 3
DETOUR = (2, 3)
DETOUR_ROWS = 64
ENDS = 2 * LINE - 1
BACK = (ENDS - 1, ENDS - 2 * HOP, ENDS - 4 * HOP, 0)
FORTH = tuple(ENDS - spot for spot in BACK)
STORE_ROWS = 128


def finish(wide, raw, inverse):
    unit = raw.astype(jnp.float32) * inverse
    along = jnp.sum(unit * wide, axis=1, keepdims=True)
    return (inverse * (wide - unit * along)).astype(jnp.bfloat16)


def finish_kernel(
    u_out, v_grad, v_raw, v_inv, last_unit, last_weights, gi_ref, gt_ref, v_out, u_sem, v_sem
):
    core = lax.rem(lax.axis_index("dp"), 2)
    slots = v_grad.shape[0] // STORE_ROWS

    @pl.when(core == 0)
    def _():
        pltpu.make_async_copy(u_out, gt_ref, u_sem).start()

    @pl.when(core == 1)
    def _():
        pltpu.make_async_copy(u_out, gi_ref, u_sem).start()

    for slot in range(slots):
        part = pl.ds(slot * STORE_ROWS, STORE_ROWS)
        wide = v_grad[part, :] + jnp.dot(
            last_weights[part, :], last_unit[...], preferred_element_type=jnp.float32
        )
        v_out[part, :] = finish(wide, v_raw[part, :], v_inv[part, 0:1])

        @pl.when(core == 0)
        def _():
            pltpu.make_async_copy(v_out.at[part], gi_ref.at[part], v_sem.at[slot]).start()

        @pl.when(core == 1)
        def _():
            pltpu.make_async_copy(v_out.at[part], gt_ref.at[part], v_sem.at[slot]).start()

    pltpu.make_async_copy(u_out, gt_ref, u_sem).wait()
    for slot in range(slots):
        part = pl.ds(slot * STORE_ROWS, STORE_ROWS)
        pltpu.make_async_copy(v_out.at[part], gi_ref.at[part], v_sem.at[slot]).wait()


def kernel(
    n,
    img_ref,
    txt_ref,
    scale_ref,
    bias_ref,
    u_out,
    v_grad,
    v_raw,
    v_inv,
    last_unit,
    last_weights,
    scale_here,
    bias_here,
    u_raw,
    chip_raw,
    near_raw,
    relay_raw,
    far_raw,
    u_unit,
    v_unit,
    block_unit,
    u_inv,
    u_grad,
    load_sem,
    chip_send,
    chip_recv,
    near_send,
    near_recv,
    relay_send,
    relay_recv,
    far_send,
    far_recv,
    detour_raw,
    detour_send,
    detour_recv,
    ready,
):
    rows, depth = u_raw.shape
    me = lax.axis_index("dp")
    core = lax.rem(me, 2)
    partner = me + 1 - 2 * core
    near_to = lax.rem(me + 4 * core - 2 + n, n)
    far_to = lax.rem(me + 2 * core - 1 + n, n)
    spot = lax.rem(me, 2 * LINE)
    sign = 2 * core - 1

    def away(by):
        return lax.rem(me + by + n, n)

    leaves = jnp.logical_or(spot >= ENDS - 1, spot == BACK[1])
    from_last = jnp.logical_and(me >= n - 2 * LINE, leaves)
    to_first = jnp.logical_and(me < 2 * LINE, jnp.logical_not(leaves))
    back = jnp.where(jnp.logical_or(from_last, to_first), -1, spot)

    def any_of(*conditions):
        return functools.reduce(jnp.logical_or, conditions)

    def back_at(*steps):
        return any_of(*[back == BACK[step] for step in steps])

    def forth_at(*steps):
        return any_of(*[spot == FORTH[step] for step in steps])

    lead_to = away(sign * (2 * HOP - 1))
    hop_to = away(sign * (4 * HOP - 2))
    home_to = away(-sign * HOP)
    steps = (2 * HOP - 1, 2 - 4 * HOP, HOP)
    skips = jnp.logical_or(back == FORTH[3], spot == BACK[3])
    detours = jnp.logical_or(back_at(0, 1, 2), forth_at(0, 1, 2))

    barrier = pltpu.get_barrier_semaphore()
    near_from = lax.rem(me + 2 - 4 * core + n, n)
    for sender in (partner, near_from, far_to):
        pl.semaphore_signal(barrier, inc=1, device_id=(sender,), device_id_type=MESH)
    for step, by in enumerate(steps):

        @pl.when(back_at(step + 1))
        def _():
            pl.semaphore_signal(barrier, inc=1, device_id=(away(by),), device_id_type=MESH)

        @pl.when(forth_at(step) if step < 2 else forth_at(3))
        def _():
            pl.semaphore_signal(
                barrier,
                inc=1,
                device_id=(away(by if step < 2 else -by),),
                device_id_type=MESH,
            )

    extra = [back_at(0), back_at(1), back_at(2), forth_at(1), forth_at(2), forth_at(2)]
    signals = 3 + sum(one.astype(jnp.int32) for one in extra)

    load_scale = pltpu.make_async_copy(scale_ref, scale_here, load_sem.at[2])
    load_bias = pltpu.make_async_copy(bias_ref, bias_here, load_sem.at[3])
    load_scale.start()
    load_bias.start()

    def on_core(which, u_source, v_source):
        @pl.when(core == which)
        def _():
            load_u = pltpu.make_async_copy(u_source, u_raw, load_sem.at[0])
            load_v = pltpu.make_async_copy(v_source, v_raw, load_sem.at[1])
            load_u.start()
            load_v.start()
            pl.semaphore_wait(barrier, signals)
            for by, receiver in zip(steps, FORTH[1:3]):
                if receiver % 2 == which:

                    @pl.when(spot == receiver)
                    def _():
                        pl.semaphore_signal(
                            ready, inc=1, device_id=(away(-by),), device_id_type=MESH
                        )

            def lead():
                for j, k in enumerate(DETOUR):
                    send_detour(u_source.at[pl.ds(*FAR_CHUNKS[k])], j, lead_to).start()

            if which == BACK[0] % 2:
                pl.when(back_at(0))(lead)
            send_chip(u_source).start()
            nears = rows // NEAR_ROWS
            for k in range(nears):
                if which == FORTH[0] % 2 and k == nears // 2:

                    @pl.when(spot == FORTH[0])
                    def _():
                        pl.semaphore_wait(ready, 1)
                        lead()

                send_near(v_source, k).start()

    def send_chip(source):
        return pltpu.make_async_remote_copy(
            src_ref=source,
            dst_ref=chip_raw,
            send_sem=chip_send.at[0],
            recv_sem=chip_recv.at[0],
            device_id=(partner,),
            device_id_type=MESH,
        )

    def send_near(source, k):
        part = pl.ds(k * NEAR_ROWS, NEAR_ROWS)
        return pltpu.make_async_remote_copy(
            src_ref=source.at[part],
            dst_ref=near_raw.at[part],
            send_sem=near_send.at[k],
            recv_sem=near_recv.at[k],
            device_id=(near_to,),
            device_id_type=MESH,
        )

    def send_relay(k):
        part = pl.ds(k * NEAR_ROWS, NEAR_ROWS)
        return pltpu.make_async_remote_copy(
            src_ref=near_raw.at[part],
            dst_ref=relay_raw.at[part],
            send_sem=relay_send.at[k],
            recv_sem=relay_recv.at[k],
            device_id=(partner,),
            device_id_type=MESH,
        )

    def send_far(k):
        part = pl.ds(*FAR_CHUNKS[k])
        return pltpu.make_async_remote_copy(
            src_ref=chip_raw.at[part],
            dst_ref=far_raw.at[part],
            send_sem=far_send.at[k],
            recv_sem=far_recv.at[k],
            device_id=(far_to,),
            device_id_type=MESH,
        )

    def send_detour(source, j, to):
        return pltpu.make_async_remote_copy(
            src_ref=source,
            dst_ref=detour_raw.at[pl.ds(j * DETOUR_ROWS, DETOUR_ROWS)],
            send_sem=detour_send.at[j],
            recv_sem=detour_recv.at[j],
            device_id=(to,),
            device_id_type=MESH,
        )

    def pass_detour(j, hop):
        held = detour_raw.at[pl.ds(j * DETOUR_ROWS, DETOUR_ROWS)]

        @pl.when(jnp.logical_or(back_at(hop), forth_at(hop)))
        def _():
            if j == 0 and hop == 1:

                @pl.when(spot == FORTH[hop])
                def _():
                    pl.semaphore_wait(ready, 1)

            send_detour(held, j, hop_to).wait_recv()
            if hop == 1:
                send_detour(held, j, hop_to).start()
            else:
                k = DETOUR[j]
                pltpu.make_async_remote_copy(
                    src_ref=held,
                    dst_ref=far_raw.at[pl.ds(*FAR_CHUNKS[k])],
                    send_sem=detour_send.at[j],
                    recv_sem=far_recv.at[k],
                    device_id=(home_to,),
                    device_id_type=MESH,
                ).start()

    on_core(0, txt_ref, img_ref)
    on_core(1, img_ref, txt_ref)

    def normalize(raw, unit, start, count, inverses=None):
        for at in range(start, start + count, 64):
            part = pl.ds(at, min(64, count))
            wide = raw[part, :].astype(jnp.float32)
            inverse = lax.rsqrt(jnp.sum(wide * wide, axis=1, keepdims=True) + EPS)
            unit[part, :] = (wide * inverse).astype(jnp.bfloat16)
            if inverses is not None:
                inverses[part, :] = jnp.broadcast_to(inverse, (part.size, inverses.shape[1]))

    def weigh(own, part, diagonal=False):
        logits = scale * lax.dot_general(
            own, part, (((1,), (1,)), ((), ())), preferred_element_type=jnp.float32
        ) + bias
        if diagonal:
            down = lax.broadcasted_iota(jnp.int32, logits.shape, 0)
            across = lax.broadcasted_iota(jnp.int32, logits.shape, 1)
            signs = jnp.where(down == across, jnp.float32(1.0), jnp.float32(-1.0))
            slope = -signs * jax.nn.sigmoid(-signs * logits)
        else:
            slope = jax.nn.sigmoid(logits)
        return (scale * slope).astype(jnp.bfloat16)

    def accumulate(own, block, start, count, grad, diagonal=False, first=False):
        part = block[pl.ds(start, count), :]
        for at in range(0, rows, TILE):
            here = pl.ds(at, TILE)
            weights = weigh(own[here, :], part, diagonal and at == start)
            term = jnp.dot(weights, part, preferred_element_type=jnp.float32)
            grad[here, :] = term if first else grad[here, :] + term

    pltpu.make_async_copy(txt_ref, u_raw, load_sem.at[0]).wait()
    pltpu.make_async_copy(img_ref, v_raw, load_sem.at[1]).wait()
    normalize(u_raw, u_unit, 0, rows, u_inv)
    normalize(v_raw, v_unit, 0, rows, v_inv)
    load_scale.wait()
    load_bias.wait()
    scale = scale_here[0]
    bias = bias_here[0]
    for start in range(0, rows, TILE):
        accumulate(u_unit, v_unit, start, TILE, u_grad, diagonal=True, first=start == 0)
        accumulate(v_unit, u_unit, start, TILE, v_grad, diagonal=True, first=start == 0)

    send_chip(txt_ref).wait_recv()
    fars = len(FAR_CHUNKS)
    for k in range(fars):
        if k in DETOUR:
            pl.when(jnp.logical_not(skips))(send_far(k).start)
        else:
            send_far(k).start()

    normalize(chip_raw, block_unit, 0, rows)
    for start in range(0, rows, TILE):
        accumulate(u_unit, block_unit, start, TILE, u_grad)

    per_tile = TILE // NEAR_ROWS
    nears = rows // NEAR_ROWS

    def take_relay():
        for tile in range(rows // TILE):
            for k in range(tile * per_tile, (tile + 1) * per_tile):
                send_relay(k).wait_recv()
                normalize(relay_raw, block_unit, k * NEAR_ROWS, NEAR_ROWS)
            accumulate(v_unit, block_unit, tile * TILE, TILE, v_grad)

    near_late = spot == FORTH[0]
    pl.when(near_late)(take_relay)
    for tile in range(rows // TILE):
        for k in range(tile * per_tile, (tile + 1) * per_tile):
            send_near(img_ref, k).wait_recv()
            send_relay(k).start()
            if k % 2 == 0:
                pass_detour(k // 2, 1)
            normalize(near_raw, block_unit, k * NEAR_ROWS, NEAR_ROWS)
        accumulate(u_unit, block_unit, tile * TILE, TILE, u_grad)
    pl.when(jnp.logical_not(near_late))(take_relay)
    for at in range(0, rows, 64):
        here = pl.ds(at, 64)
        u_out[here, :] = finish(u_grad[here, :], u_raw[here, :], u_inv[here, 0:1])

    for g, chunks in enumerate(FAR_GROUPS):
        for j in ((0, 1), (), (), ())[g]:
            pass_detour(j, 2)
        for k in chunks:
            send_far(k).wait_recv()
        start = FAR_CHUNKS[chunks[0]][0]
        count = sum(FAR_CHUNKS[k][1] for k in chunks)
        normalize(far_raw, block_unit, start, count)
        if g + 1 < len(FAR_GROUPS):
            accumulate(v_unit, block_unit, start, count, v_grad)
        else:
            last_unit[...] = block_unit[pl.ds(start, count), :]
            for at in range(0, rows, TILE):
                here = pl.ds(at, TILE)
                last_weights[here, :] = weigh(v_unit[here, :], last_unit[...])

    for k in range(nears):
        send_near(img_ref, k).wait_send()
        send_relay(k).wait_send()
    for k in range(fars):
        if k in DETOUR:
            pl.when(jnp.logical_not(skips))(send_far(k).wait_send)
        else:
            send_far(k).wait_send()

    @pl.when(detours)
    def _():
        for j in range(len(DETOUR)):
            send_detour(detour_raw.at[pl.ds(j * DETOUR_ROWS, DETOUR_ROWS)], j, hop_to).wait_send()

    send_chip(txt_ref).wait_send()


def solution(mesh):
    n = mesh.shape["dp"]

    def shards(images, texts, logit_scale, logit_bias):
        rows, depth = images.shape
        block = pltpu.VMEM((rows, depth), jnp.bfloat16)
        total = pltpu.VMEM((rows, depth), jnp.float32)
        inverses = pltpu.VMEM((rows, 128), jnp.float32)
        dma = pltpu.SemaphoreType.DMA
        nears, fars = rows // NEAR_ROWS, len(FAR_CHUNKS)
        scalar = pltpu.SMEM((1,), jnp.float32)
        last = pltpu.VMEM((LAST_ROWS, depth), jnp.bfloat16)
        last_weights = pltpu.VMEM((rows, LAST_ROWS), jnp.bfloat16)
        in_vmem = pl.BlockSpec(memory_space=pltpu.VMEM)
        in_hbm = pl.BlockSpec(memory_space=pltpu.HBM)
        operands = [
            pltpu.with_memory_space_constraint(operand, pltpu.HBM)
            for operand in (images, texts)
        ]
        parts = pl.pallas_call(
            functools.partial(kernel, n),
            out_shape=(block, total, block, inverses, last, last_weights),
            in_specs=[in_hbm] * 2 + [pl.BlockSpec(memory_space=pl.ANY)] * 2,
            out_specs=[in_vmem] * 6,
            scratch_shapes=[scalar] * 2
            + [block] * 5
            + [block] * 3
            + [inverses]
            + [total]
            + [
                dma((4,)),
                dma((1,)),
                dma((1,)),
                dma((nears,)),
                dma((nears,)),
                dma((nears,)),
                dma((nears,)),
                dma((fars,)),
                dma((fars,)),
                pltpu.VMEM((len(DETOUR) * DETOUR_ROWS, depth), jnp.bfloat16),
                dma((len(DETOUR),)),
                dma((len(DETOUR),)),
                pltpu.SemaphoreType.REGULAR,
            ],
            compiler_params=pltpu.CompilerParams(
                collective_id=0, has_side_effects=True, vmem_limit_bytes=40 * 1024 * 1024
            ),
            cost_estimate=pl.CostEstimate(
                flops=24 * rows * rows * depth, bytes_accessed=8 * rows * depth, transcendentals=0
            ),
        )(*operands, logit_scale, logit_bias)
        parts = [pltpu.with_memory_space_constraint(part, pltpu.VMEM) for part in parts]
        result = jax.ShapeDtypeStruct((rows, depth), jnp.bfloat16)
        return pl.pallas_call(
            finish_kernel,
            out_shape=(result, result),
            in_specs=[in_vmem] * 6,
            out_specs=[in_hbm] * 2,
            scratch_shapes=[block, dma, dma((rows // STORE_ROWS,))],
            compiler_params=pltpu.CompilerParams(vmem_limit_bytes=16 * 1024 * 1024),
            cost_estimate=pl.CostEstimate(
                flops=8 * rows * depth, bytes_accessed=4 * rows * depth, transcendentals=0
            ),
        )(*parts)

    in_specs = (P("dp", None), P("dp", None), P(), P())
    out_specs = (P("dp", None), P("dp", None))
    return jax.shard_map(shards, mesh=mesh, in_specs=in_specs, out_specs=out_specs, check_vma=False)
```

```python
import functools

import jax
import jax.numpy as jnp
from jax import lax
from jax.experimental import pallas as pl
from jax.experimental.pallas import tpu as pltpu
from jax.sharding import PartitionSpec as P

EPS = 1e-06
MESH = pl.DeviceIdType.MESH
TILE = 256
NEAR_ROWS = 128
FAR_CHUNKS = ((0, 128), (128, 96), (224, 80), (304, 80), (384, 64), (448, 64))
FAR_GROUPS = ((0,), (1,), (2, 3, 4), (5,))
LAST_ROWS = FAR_CHUNKS[-1][1]
LINE = 8
HOP = 3
DETOUR = (2, 3)
DETOUR_ROWS = 80
ENDS = 2 * LINE - 1
BACK = (ENDS - 1, ENDS - 2 * HOP, ENDS - 4 * HOP, 0)
FORTH = tuple(ENDS - spot for spot in BACK)
STORE_ROWS = 128


def finish(wide, raw, inverse):
    unit = raw.astype(jnp.float32) * inverse
    along = jnp.sum(unit * wide, axis=1, keepdims=True)
    return (inverse * (wide - unit * along)).astype(jnp.bfloat16)


def finish_kernel(
    u_out, v_grad, v_raw, v_inv, last_unit, last_weights, gi_ref, gt_ref, v_out, u_sem, v_sem
):
    core = lax.rem(lax.axis_index("dp"), 2)
    slots = v_grad.shape[0] // STORE_ROWS

    @pl.when(core == 0)
    def _():
        pltpu.make_async_copy(u_out, gt_ref, u_sem).start()

    @pl.when(core == 1)
    def _():
        pltpu.make_async_copy(u_out, gi_ref, u_sem).start()

    for slot in range(slots):
        part = pl.ds(slot * STORE_ROWS, STORE_ROWS)
        wide = v_grad[part, :] + jnp.dot(
            last_weights[part, :], last_unit[...], preferred_element_type=jnp.float32
        )
        v_out[part, :] = finish(wide, v_raw[part, :], v_inv[part, 0:1])

        @pl.when(core == 0)
        def _():
            pltpu.make_async_copy(v_out.at[part], gi_ref.at[part], v_sem.at[slot]).start()

        @pl.when(core == 1)
        def _():
            pltpu.make_async_copy(v_out.at[part], gt_ref.at[part], v_sem.at[slot]).start()

    pltpu.make_async_copy(u_out, gt_ref, u_sem).wait()
    for slot in range(slots):
        part = pl.ds(slot * STORE_ROWS, STORE_ROWS)
        pltpu.make_async_copy(v_out.at[part], gi_ref.at[part], v_sem.at[slot]).wait()


def kernel(
    n,
    img_ref,
    txt_ref,
    scale_ref,
    bias_ref,
    u_out,
    v_grad,
    v_raw,
    v_inv,
    last_unit,
    last_weights,
    scale_here,
    bias_here,
    u_raw,
    chip_raw,
    near_raw,
    relay_raw,
    far_raw,
    u_unit,
    v_unit,
    block_unit,
    u_inv,
    u_grad,
    load_sem,
    chip_send,
    chip_recv,
    near_send,
    near_recv,
    relay_send,
    relay_recv,
    far_send,
    far_recv,
    detour_raw,
    detour_send,
    detour_recv,
    ready,
    mate,
):
    rows, depth = u_raw.shape
    me = lax.axis_index("dp")
    core = lax.rem(me, 2)
    partner = me + 1 - 2 * core
    near_to = lax.rem(me + 4 * core - 2 + n, n)
    far_to = lax.rem(me + 2 * core - 1 + n, n)
    spot = lax.rem(me, 2 * LINE)
    sign = 2 * core - 1

    def away(by):
        return lax.rem(me + by + n, n)

    leaves = jnp.logical_or(spot >= ENDS - 1, spot == BACK[1])
    from_last = jnp.logical_and(me >= n - 2 * LINE, leaves)
    to_first = jnp.logical_and(me < 2 * LINE, jnp.logical_not(leaves))
    back = jnp.where(jnp.logical_or(from_last, to_first), -1, spot)

    def any_of(*conditions):
        return functools.reduce(jnp.logical_or, conditions)

    def back_at(*steps):
        return any_of(*[back == BACK[step] for step in steps])

    def forth_at(*steps):
        return any_of(*[spot == FORTH[step] for step in steps])

    lead_to = away(sign * (2 * HOP - 1))
    hop_to = away(sign * (4 * HOP - 2))
    home_to = away(-sign * HOP)
    steps = (2 * HOP - 1, 2 - 4 * HOP, HOP)
    skips = jnp.logical_or(back == FORTH[3], spot == BACK[3])
    detours = jnp.logical_or(back_at(0, 1, 2), forth_at(0, 1, 2))

    barrier = pltpu.get_barrier_semaphore()
    near_from = lax.rem(me + 2 - 4 * core + n, n)
    @pl.when(core == 1)
    def _():
        pl.semaphore_signal(barrier, inc=1, device_id=(partner,), device_id_type=MESH)

    for sender in (near_from, far_to):
        pl.semaphore_signal(barrier, inc=1, device_id=(sender,), device_id_type=MESH)
    for step, by in enumerate(steps):

        @pl.when(back_at(step + 1))
        def _():
            pl.semaphore_signal(barrier, inc=1, device_id=(away(by),), device_id_type=MESH)

        @pl.when(forth_at(step) if step < 2 else forth_at(3))
        def _():
            pl.semaphore_signal(
                barrier,
                inc=1,
                device_id=(away(by if step < 2 else -by),),
                device_id_type=MESH,
            )

    extra = [back_at(0), back_at(1), back_at(2), forth_at(1), forth_at(2), forth_at(2)]
    signals = 3 - core + sum(one.astype(jnp.int32) for one in extra)

    load_scale = pltpu.make_async_copy(scale_ref, scale_here, load_sem.at[2])
    load_bias = pltpu.make_async_copy(bias_ref, bias_here, load_sem.at[3])
    load_scale.start()
    load_bias.start()

    def on_core(which, u_source, v_source):
        @pl.when(core == which)
        def _():
            load_u = pltpu.make_async_copy(u_source, u_raw, load_sem.at[0])
            load_v = pltpu.make_async_copy(v_source, v_raw, load_sem.at[1])
            load_u.start()
            load_v.start()
            pl.semaphore_wait(barrier, signals)
            for by, receiver in zip(steps, FORTH[1:3]):
                if receiver % 2 == which:

                    @pl.when(spot == receiver)
                    def _():
                        pl.semaphore_signal(
                            ready, inc=1, device_id=(away(-by),), device_id_type=MESH
                        )

            def lead():
                for j, k in enumerate(DETOUR):
                    send_detour(u_source.at[pl.ds(*FAR_CHUNKS[k])], j, lead_to).start()

            if which == BACK[0] % 2:
                pl.when(back_at(0))(lead)
            if which == 0:
                pl.semaphore_signal(mate, inc=1, device_id=(partner,), device_id_type=MESH)
                send_chip(u_source).start()
            nears = rows // NEAR_ROWS
            for k in range(nears):
                if which == FORTH[0] % 2 and k == nears // 2:

                    @pl.when(spot == FORTH[0])
                    def _():
                        pl.semaphore_wait(ready, 1)
                        lead()

                send_near(v_source, k).start()

    def send_chip(source):
        return pltpu.make_async_remote_copy(
            src_ref=source,
            dst_ref=chip_raw,
            send_sem=chip_send.at[0],
            recv_sem=chip_recv.at[0],
            device_id=(partner,),
            device_id_type=MESH,
        )

    def send_near(source, k):
        part = pl.ds(k * NEAR_ROWS, NEAR_ROWS)
        return pltpu.make_async_remote_copy(
            src_ref=source.at[part],
            dst_ref=near_raw.at[part],
            send_sem=near_send.at[k],
            recv_sem=near_recv.at[k],
            device_id=(near_to,),
            device_id_type=MESH,
        )

    def send_relay(k):
        part = pl.ds(k * NEAR_ROWS, NEAR_ROWS)
        return pltpu.make_async_remote_copy(
            src_ref=near_raw.at[part],
            dst_ref=relay_raw.at[part],
            send_sem=relay_send.at[k],
            recv_sem=relay_recv.at[k],
            device_id=(partner,),
            device_id_type=MESH,
        )

    def send_far(k):
        part = pl.ds(*FAR_CHUNKS[k])
        return pltpu.make_async_remote_copy(
            src_ref=chip_raw.at[part],
            dst_ref=far_raw.at[part],
            send_sem=far_send.at[k],
            recv_sem=far_recv.at[k],
            device_id=(far_to,),
            device_id_type=MESH,
        )

    def send_detour(source, j, to):
        return pltpu.make_async_remote_copy(
            src_ref=source,
            dst_ref=detour_raw.at[pl.ds(j * DETOUR_ROWS, DETOUR_ROWS)],
            send_sem=detour_send.at[j],
            recv_sem=detour_recv.at[j],
            device_id=(to,),
            device_id_type=MESH,
        )

    def pass_detour(j, hop):
        held = detour_raw.at[pl.ds(j * DETOUR_ROWS, DETOUR_ROWS)]

        @pl.when(jnp.logical_or(back_at(hop), forth_at(hop)))
        def _():
            if j == 0 and hop == 1:

                @pl.when(spot == FORTH[hop])
                def _():
                    pl.semaphore_wait(ready, 1)

            send_detour(held, j, hop_to).wait_recv()
            if hop == 1:
                send_detour(held, j, hop_to).start()
            else:
                k = DETOUR[j]
                pltpu.make_async_remote_copy(
                    src_ref=held,
                    dst_ref=far_raw.at[pl.ds(*FAR_CHUNKS[k])],
                    send_sem=detour_send.at[j],
                    recv_sem=far_recv.at[k],
                    device_id=(home_to,),
                    device_id_type=MESH,
                ).start()

    on_core(0, txt_ref, img_ref)
    on_core(1, img_ref, txt_ref)

    def normalize(raw, unit, start, count, inverses=None):
        step = 64 if count % 64 == 0 else 32
        for at in range(start, start + count, step):
            part = pl.ds(at, step)
            wide = raw[part, :].astype(jnp.float32)
            inverse = lax.rsqrt(jnp.sum(wide * wide, axis=1, keepdims=True) + EPS)
            unit[part, :] = (wide * inverse).astype(jnp.bfloat16)
            if inverses is not None:
                inverses[part, :] = jnp.broadcast_to(inverse, (part.size, inverses.shape[1]))

    def weigh(own, part, diagonal=False):
        logits = scale * lax.dot_general(
            own, part, (((1,), (1,)), ((), ())), preferred_element_type=jnp.float32
        ) + bias
        if diagonal:
            down = lax.broadcasted_iota(jnp.int32, logits.shape, 0)
            across = lax.broadcasted_iota(jnp.int32, logits.shape, 1)
            signs = jnp.where(down == across, jnp.float32(1.0), jnp.float32(-1.0))
            slope = -signs * jax.nn.sigmoid(-signs * logits)
        else:
            slope = jax.nn.sigmoid(logits)
        return (scale * slope).astype(jnp.bfloat16)

    def accumulate(own, block, start, count, grad, diagonal=False, first=False):
        part = block[pl.ds(start, count), :]
        for at in range(0, rows, TILE):
            here = pl.ds(at, TILE)
            weights = weigh(own[here, :], part, diagonal and at == start)
            term = jnp.dot(weights, part, preferred_element_type=jnp.float32)
            grad[here, :] = term if first else grad[here, :] + term

    pltpu.make_async_copy(txt_ref, u_raw, load_sem.at[0]).wait()
    pltpu.make_async_copy(img_ref, v_raw, load_sem.at[1]).wait()
    normalize(u_raw, u_unit, 0, rows, u_inv)
    normalize(v_raw, v_unit, 0, rows, v_inv)
    load_scale.wait()
    load_bias.wait()
    scale = scale_here[0]
    bias = bias_here[0]
    for start in range(0, rows, TILE):
        accumulate(u_unit, v_unit, start, TILE, u_grad, diagonal=True, first=start == 0)
        accumulate(v_unit, u_unit, start, TILE, v_grad, diagonal=True, first=start == 0)

    @pl.when(core == 1)
    def _():
        pl.semaphore_wait(mate, 1)
        send_chip(img_ref).start()

    send_chip(txt_ref).wait_recv()
    fars = len(FAR_CHUNKS)
    for k in range(fars):
        if k in DETOUR:
            pl.when(jnp.logical_not(skips))(send_far(k).start)
        else:
            send_far(k).start()

    normalize(chip_raw, block_unit, 0, rows)
    for start in range(0, rows, TILE):
        accumulate(u_unit, block_unit, start, TILE, u_grad)

    per_tile = TILE // NEAR_ROWS
    nears = rows // NEAR_ROWS

    def take_relay():
        for tile in range(rows // TILE):
            for k in range(tile * per_tile, (tile + 1) * per_tile):
                send_relay(k).wait_recv()
                normalize(relay_raw, block_unit, k * NEAR_ROWS, NEAR_ROWS)
            accumulate(v_unit, block_unit, tile * TILE, TILE, v_grad)

    near_late = spot == FORTH[0]
    pl.when(near_late)(take_relay)
    for tile in range(rows // TILE):
        for k in range(tile * per_tile, (tile + 1) * per_tile):
            send_near(img_ref, k).wait_recv()
            send_relay(k).start()
            if k % 2 == 0:
                pass_detour(k // 2, 1)
            normalize(near_raw, block_unit, k * NEAR_ROWS, NEAR_ROWS)
        accumulate(u_unit, block_unit, tile * TILE, TILE, u_grad)
    pl.when(jnp.logical_not(near_late))(take_relay)
    for at in range(0, rows, 64):
        here = pl.ds(at, 64)
        u_out[here, :] = finish(u_grad[here, :], u_raw[here, :], u_inv[here, 0:1])

    for g, chunks in enumerate(FAR_GROUPS):
        for j in ((0, 1), (), (), ())[g]:
            pass_detour(j, 2)
        for k in chunks:
            send_far(k).wait_recv()
        start = FAR_CHUNKS[chunks[0]][0]
        count = sum(FAR_CHUNKS[k][1] for k in chunks)
        normalize(far_raw, block_unit, start, count)
        if g + 1 < len(FAR_GROUPS):
            accumulate(v_unit, block_unit, start, count, v_grad)
        else:
            last_unit[...] = block_unit[pl.ds(start, count), :]
            for at in range(0, rows, TILE):
                here = pl.ds(at, TILE)
                last_weights[here, :] = weigh(v_unit[here, :], last_unit[...])

    for k in range(nears):
        send_near(img_ref, k).wait_send()
        send_relay(k).wait_send()
    for k in range(fars):
        if k in DETOUR:
            pl.when(jnp.logical_not(skips))(send_far(k).wait_send)
        else:
            send_far(k).wait_send()

    @pl.when(detours)
    def _():
        for j in range(len(DETOUR)):
            send_detour(detour_raw.at[pl.ds(j * DETOUR_ROWS, DETOUR_ROWS)], j, hop_to).wait_send()

    send_chip(txt_ref).wait_send()


def solution(mesh):
    n = mesh.shape["dp"]

    def shards(images, texts, logit_scale, logit_bias):
        rows, depth = images.shape
        block = pltpu.VMEM((rows, depth), jnp.bfloat16)
        total = pltpu.VMEM((rows, depth), jnp.float32)
        inverses = pltpu.VMEM((rows, 128), jnp.float32)
        dma = pltpu.SemaphoreType.DMA
        nears, fars = rows // NEAR_ROWS, len(FAR_CHUNKS)
        scalar = pltpu.SMEM((1,), jnp.float32)
        last = pltpu.VMEM((LAST_ROWS, depth), jnp.bfloat16)
        last_weights = pltpu.VMEM((rows, LAST_ROWS), jnp.bfloat16)
        in_vmem = pl.BlockSpec(memory_space=pltpu.VMEM)
        in_hbm = pl.BlockSpec(memory_space=pltpu.HBM)
        operands = [
            pltpu.with_memory_space_constraint(operand, pltpu.HBM)
            for operand in (images, texts)
        ]
        parts = pl.pallas_call(
            functools.partial(kernel, n),
            out_shape=(block, total, block, inverses, last, last_weights),
            in_specs=[in_hbm] * 2 + [pl.BlockSpec(memory_space=pl.ANY)] * 2,
            out_specs=[in_vmem] * 6,
            scratch_shapes=[scalar] * 2
            + [block] * 5
            + [block] * 3
            + [inverses]
            + [total]
            + [
                dma((4,)),
                dma((1,)),
                dma((1,)),
                dma((nears,)),
                dma((nears,)),
                dma((nears,)),
                dma((nears,)),
                dma((fars,)),
                dma((fars,)),
                pltpu.VMEM((len(DETOUR) * DETOUR_ROWS, depth), jnp.bfloat16),
                dma((len(DETOUR),)),
                dma((len(DETOUR),)),
                pltpu.SemaphoreType.REGULAR,
                pltpu.SemaphoreType.REGULAR,
            ],
            compiler_params=pltpu.CompilerParams(
                collective_id=0, has_side_effects=True, vmem_limit_bytes=40 * 1024 * 1024
            ),
            cost_estimate=pl.CostEstimate(
                flops=24 * rows * rows * depth, bytes_accessed=8 * rows * depth, transcendentals=0
            ),
        )(*operands, logit_scale, logit_bias)
        parts = [pltpu.with_memory_space_constraint(part, pltpu.VMEM) for part in parts]
        result = jax.ShapeDtypeStruct((rows, depth), jnp.bfloat16)
        return pl.pallas_call(
            finish_kernel,
            out_shape=(result, result),
            in_specs=[in_vmem] * 6,
            out_specs=[in_hbm] * 2,
            scratch_shapes=[block, dma, dma((rows // STORE_ROWS,))],
            compiler_params=pltpu.CompilerParams(vmem_limit_bytes=16 * 1024 * 1024),
            cost_estimate=pl.CostEstimate(
                flops=8 * rows * depth, bytes_accessed=4 * rows * depth, transcendentals=0
            ),
        )(*parts)

    in_specs = (P("dp", None), P("dp", None), P(), P())
    out_specs = (P("dp", None), P("dp", None))
    return jax.shard_map(shards, mesh=mesh, in_specs=in_specs, out_specs=out_specs, check_vma=False)
```

```python
import functools

import jax
import jax.numpy as jnp
from jax import lax
from jax.experimental import pallas as pl
from jax.experimental.pallas import tpu as pltpu
from jax.sharding import PartitionSpec as P

EPS = 1e-06
MESH = pl.DeviceIdType.MESH
TILE = 256
NEAR_ROWS = 128
FAR_CHUNKS = ((0, 128), (128, 96), (224, 80), (304, 80), (384, 64), (448, 64))
FAR_GROUPS = ((0, 1), (2, 3, 4), (5,))
LAST_ROWS = FAR_CHUNKS[-1][1]
LINE = 8
HOP = 3
DETOUR = (2, 3)
DETOUR_ROWS = 80
ENDS = 2 * LINE - 1
BACK = (ENDS - 1, ENDS - 2 * HOP, ENDS - 4 * HOP, 0)
FORTH = tuple(ENDS - spot for spot in BACK)
STORE_ROWS = 128


def finish(wide, raw, inverse):
    unit = raw.astype(jnp.float32) * inverse
    along = jnp.sum(unit * wide, axis=1, keepdims=True)
    return (inverse * (wide - unit * along)).astype(jnp.bfloat16)


def finish_kernel(
    u_out, v_grad, v_raw, v_inv, last_unit, last_weights, gi_ref, gt_ref, v_out, u_sem, v_sem
):
    core = lax.rem(lax.axis_index("dp"), 2)
    slots = v_grad.shape[0] // STORE_ROWS

    @pl.when(core == 0)
    def _():
        pltpu.make_async_copy(u_out, gt_ref, u_sem).start()

    @pl.when(core == 1)
    def _():
        pltpu.make_async_copy(u_out, gi_ref, u_sem).start()

    for slot in range(slots):
        part = pl.ds(slot * STORE_ROWS, STORE_ROWS)
        wide = v_grad[part, :] + jnp.dot(
            last_weights[part, :], last_unit[...], preferred_element_type=jnp.float32
        )
        v_out[part, :] = finish(wide, v_raw[part, :], v_inv[part, 0:1])

        @pl.when(core == 0)
        def _():
            pltpu.make_async_copy(v_out.at[part], gi_ref.at[part], v_sem.at[slot]).start()

        @pl.when(core == 1)
        def _():
            pltpu.make_async_copy(v_out.at[part], gt_ref.at[part], v_sem.at[slot]).start()

    pltpu.make_async_copy(u_out, gt_ref, u_sem).wait()
    for slot in range(slots):
        part = pl.ds(slot * STORE_ROWS, STORE_ROWS)
        pltpu.make_async_copy(v_out.at[part], gi_ref.at[part], v_sem.at[slot]).wait()


def kernel(
    n,
    img_ref,
    txt_ref,
    scale_ref,
    bias_ref,
    u_out,
    v_grad,
    v_raw,
    v_inv,
    last_unit,
    last_weights,
    scale_here,
    bias_here,
    u_raw,
    chip_raw,
    near_raw,
    relay_raw,
    far_raw,
    u_unit,
    v_unit,
    block_unit,
    u_inv,
    u_grad,
    load_sem,
    chip_send,
    chip_recv,
    near_send,
    near_recv,
    relay_send,
    relay_recv,
    far_send,
    far_recv,
    detour_raw,
    detour_send,
    detour_recv,
    ready,
    mate,
):
    rows, depth = u_raw.shape
    me = lax.axis_index("dp")
    core = lax.rem(me, 2)
    partner = me + 1 - 2 * core
    near_to = lax.rem(me + 4 * core - 2 + n, n)
    far_to = lax.rem(me + 2 * core - 1 + n, n)
    spot = lax.rem(me, 2 * LINE)
    sign = 2 * core - 1

    def away(by):
        return lax.rem(me + by + n, n)

    leaves = jnp.logical_or(spot >= ENDS - 1, spot == BACK[1])
    from_last = jnp.logical_and(me >= n - 2 * LINE, leaves)
    to_first = jnp.logical_and(me < 2 * LINE, jnp.logical_not(leaves))
    back = jnp.where(jnp.logical_or(from_last, to_first), -1, spot)

    def any_of(*conditions):
        return functools.reduce(jnp.logical_or, conditions)

    def back_at(*steps):
        return any_of(*[back == BACK[step] for step in steps])

    def forth_at(*steps):
        return any_of(*[spot == FORTH[step] for step in steps])

    lead_to = away(sign * (2 * HOP - 1))
    hop_to = away(sign * (4 * HOP - 2))
    home_to = away(-sign * HOP)
    steps = (2 * HOP - 1, 2 - 4 * HOP, HOP)
    skips = jnp.logical_or(back == FORTH[3], spot == BACK[3])
    detours = jnp.logical_or(back_at(0, 1, 2), forth_at(0, 1, 2))

    barrier = pltpu.get_barrier_semaphore()
    near_from = lax.rem(me + 2 - 4 * core + n, n)
    @pl.when(core == 1)
    def _():
        pl.semaphore_signal(barrier, inc=1, device_id=(partner,), device_id_type=MESH)

    for sender in (near_from, far_to):
        pl.semaphore_signal(barrier, inc=1, device_id=(sender,), device_id_type=MESH)
    for step, by in enumerate(steps):

        @pl.when(back_at(step + 1))
        def _():
            pl.semaphore_signal(barrier, inc=1, device_id=(away(by),), device_id_type=MESH)

        @pl.when(forth_at(step) if step < 2 else forth_at(3))
        def _():
            pl.semaphore_signal(
                barrier,
                inc=1,
                device_id=(away(by if step < 2 else -by),),
                device_id_type=MESH,
            )

    extra = [back_at(0), back_at(1), back_at(2), forth_at(1), forth_at(2), forth_at(2)]
    signals = 3 - core + sum(one.astype(jnp.int32) for one in extra)

    load_scale = pltpu.make_async_copy(scale_ref, scale_here, load_sem.at[2])
    load_bias = pltpu.make_async_copy(bias_ref, bias_here, load_sem.at[3])
    load_scale.start()
    load_bias.start()

    def on_core(which, u_source, v_source):
        @pl.when(core == which)
        def _():
            load_u = pltpu.make_async_copy(u_source, u_raw, load_sem.at[0])
            load_v = pltpu.make_async_copy(v_source, v_raw, load_sem.at[1])
            load_u.start()
            load_v.start()
            pl.semaphore_wait(barrier, signals)
            for by, receiver in zip(steps, FORTH[1:3]):
                if receiver % 2 == which:

                    @pl.when(spot == receiver)
                    def _():
                        pl.semaphore_signal(
                            ready, inc=1, device_id=(away(-by),), device_id_type=MESH
                        )

            def lead():
                for j, k in enumerate(DETOUR):
                    send_detour(u_source.at[pl.ds(*FAR_CHUNKS[k])], j, lead_to).start()

            if which == BACK[0] % 2:
                pl.when(back_at(0))(lead)
            if which == 0:
                pl.semaphore_signal(mate, inc=1, device_id=(partner,), device_id_type=MESH)
                send_chip(u_source).start()
            nears = rows // NEAR_ROWS
            for k in range(nears):
                if which == FORTH[0] % 2 and k == nears // 2:

                    @pl.when(spot == FORTH[0])
                    def _():
                        pl.semaphore_wait(ready, 1)
                        lead()

                send_near(v_source, k).start()

    def send_chip(source):
        return pltpu.make_async_remote_copy(
            src_ref=source,
            dst_ref=chip_raw,
            send_sem=chip_send.at[0],
            recv_sem=chip_recv.at[0],
            device_id=(partner,),
            device_id_type=MESH,
        )

    def send_near(source, k):
        part = pl.ds(k * NEAR_ROWS, NEAR_ROWS)
        return pltpu.make_async_remote_copy(
            src_ref=source.at[part],
            dst_ref=near_raw.at[part],
            send_sem=near_send.at[k],
            recv_sem=near_recv.at[k],
            device_id=(near_to,),
            device_id_type=MESH,
        )

    def send_relay(k):
        part = pl.ds(k * NEAR_ROWS, NEAR_ROWS)
        return pltpu.make_async_remote_copy(
            src_ref=near_raw.at[part],
            dst_ref=relay_raw.at[part],
            send_sem=relay_send.at[k],
            recv_sem=relay_recv.at[k],
            device_id=(partner,),
            device_id_type=MESH,
        )

    def send_far(k):
        part = pl.ds(*FAR_CHUNKS[k])
        return pltpu.make_async_remote_copy(
            src_ref=chip_raw.at[part],
            dst_ref=far_raw.at[part],
            send_sem=far_send.at[k],
            recv_sem=far_recv.at[k],
            device_id=(far_to,),
            device_id_type=MESH,
        )

    def send_detour(source, j, to):
        return pltpu.make_async_remote_copy(
            src_ref=source,
            dst_ref=detour_raw.at[pl.ds(j * DETOUR_ROWS, DETOUR_ROWS)],
            send_sem=detour_send.at[j],
            recv_sem=detour_recv.at[j],
            device_id=(to,),
            device_id_type=MESH,
        )

    def pass_detour(j, hop):
        held = detour_raw.at[pl.ds(j * DETOUR_ROWS, DETOUR_ROWS)]

        @pl.when(jnp.logical_or(back_at(hop), forth_at(hop)))
        def _():
            if j == 0 and hop == 1:

                @pl.when(spot == FORTH[hop])
                def _():
                    pl.semaphore_wait(ready, 1)

            send_detour(held, j, hop_to).wait_recv()
            if hop == 1:
                send_detour(held, j, hop_to).start()
            else:
                k = DETOUR[j]
                pltpu.make_async_remote_copy(
                    src_ref=held,
                    dst_ref=far_raw.at[pl.ds(*FAR_CHUNKS[k])],
                    send_sem=detour_send.at[j],
                    recv_sem=far_recv.at[k],
                    device_id=(home_to,),
                    device_id_type=MESH,
                ).start()

    on_core(0, txt_ref, img_ref)
    on_core(1, img_ref, txt_ref)

    def normalize(raw, unit, start, count, inverses=None):
        step = 64 if count % 64 == 0 else 32
        for at in range(start, start + count, step):
            part = pl.ds(at, step)
            wide = raw[part, :].astype(jnp.float32)
            inverse = lax.rsqrt(jnp.sum(wide * wide, axis=1, keepdims=True) + EPS)
            unit[part, :] = (wide * inverse).astype(jnp.bfloat16)
            if inverses is not None:
                inverses[part, :] = jnp.broadcast_to(inverse, (part.size, inverses.shape[1]))

    def weigh(own, part, diagonal=False):
        logits = scale * lax.dot_general(
            own, part, (((1,), (1,)), ((), ())), preferred_element_type=jnp.float32
        ) + bias
        if diagonal:
            down = lax.broadcasted_iota(jnp.int32, logits.shape, 0)
            across = lax.broadcasted_iota(jnp.int32, logits.shape, 1)
            signs = jnp.where(down == across, jnp.float32(1.0), jnp.float32(-1.0))
            slope = -signs * jax.nn.sigmoid(-signs * logits)
        else:
            slope = jax.nn.sigmoid(logits)
        return (scale * slope).astype(jnp.bfloat16)

    def accumulate(own, block, start, count, grad, diagonal=False, first=False):
        part = block[pl.ds(start, count), :]
        for at in range(0, rows, TILE):
            here = pl.ds(at, TILE)
            weights = weigh(own[here, :], part, diagonal and at == start)
            term = jnp.dot(weights, part, preferred_element_type=jnp.float32)
            grad[here, :] = term if first else grad[here, :] + term

    pltpu.make_async_copy(txt_ref, u_raw, load_sem.at[0]).wait()
    pltpu.make_async_copy(img_ref, v_raw, load_sem.at[1]).wait()
    normalize(u_raw, u_unit, 0, rows, u_inv)
    normalize(v_raw, v_unit, 0, rows, v_inv)
    load_scale.wait()
    load_bias.wait()
    scale = scale_here[0]
    bias = bias_here[0]
    for start in range(0, rows, TILE):
        accumulate(u_unit, v_unit, start, TILE, u_grad, diagonal=True, first=start == 0)
        accumulate(v_unit, u_unit, start, TILE, v_grad, diagonal=True, first=start == 0)

    @pl.when(core == 1)
    def _():
        pl.semaphore_wait(mate, 1)
        send_chip(img_ref).start()

    send_chip(txt_ref).wait_recv()
    fars = len(FAR_CHUNKS)
    for k in range(fars):
        if k in DETOUR:
            pl.when(jnp.logical_not(skips))(send_far(k).start)
        else:
            send_far(k).start()

    normalize(chip_raw, block_unit, 0, rows)
    for start in range(0, rows, TILE):
        accumulate(u_unit, block_unit, start, TILE, u_grad)

    per_tile = TILE // NEAR_ROWS
    nears = rows // NEAR_ROWS

    def take_relay():
        for tile in range(rows // TILE):
            for k in range(tile * per_tile, (tile + 1) * per_tile):
                send_relay(k).wait_recv()
                normalize(relay_raw, block_unit, k * NEAR_ROWS, NEAR_ROWS)
            accumulate(v_unit, block_unit, tile * TILE, TILE, v_grad)

    near_late = spot == FORTH[0]
    pl.when(near_late)(take_relay)
    for tile in range(rows // TILE):
        for k in range(tile * per_tile, (tile + 1) * per_tile):
            send_near(img_ref, k).wait_recv()
            send_relay(k).start()
            if k % 2 == 0:
                pass_detour(k // 2, 1)
            normalize(near_raw, block_unit, k * NEAR_ROWS, NEAR_ROWS)
        accumulate(u_unit, block_unit, tile * TILE, TILE, u_grad)
    pl.when(jnp.logical_not(near_late))(take_relay)
    for at in range(0, rows, 64):
        here = pl.ds(at, 64)
        u_out[here, :] = finish(u_grad[here, :], u_raw[here, :], u_inv[here, 0:1])

    for g, chunks in enumerate(FAR_GROUPS):
        for j in ((0, 1), (), ())[g]:
            pass_detour(j, 2)
        for k in chunks:
            send_far(k).wait_recv()
        start = FAR_CHUNKS[chunks[0]][0]
        count = sum(FAR_CHUNKS[k][1] for k in chunks)
        normalize(far_raw, block_unit, start, count)
        if g + 1 < len(FAR_GROUPS):
            accumulate(v_unit, block_unit, start, count, v_grad)
        else:
            last_unit[...] = block_unit[pl.ds(start, count), :]
            for at in range(0, rows, TILE):
                here = pl.ds(at, TILE)
                last_weights[here, :] = weigh(v_unit[here, :], last_unit[...])

    for k in range(nears):
        send_near(img_ref, k).wait_send()
        send_relay(k).wait_send()
    for k in range(fars):
        if k in DETOUR:
            pl.when(jnp.logical_not(skips))(send_far(k).wait_send)
        else:
            send_far(k).wait_send()

    @pl.when(detours)
    def _():
        for j in range(len(DETOUR)):
            send_detour(detour_raw.at[pl.ds(j * DETOUR_ROWS, DETOUR_ROWS)], j, hop_to).wait_send()

    send_chip(txt_ref).wait_send()


def solution(mesh):
    n = mesh.shape["dp"]

    def shards(images, texts, logit_scale, logit_bias):
        rows, depth = images.shape
        block = pltpu.VMEM((rows, depth), jnp.bfloat16)
        total = pltpu.VMEM((rows, depth), jnp.float32)
        inverses = pltpu.VMEM((rows, 128), jnp.float32)
        dma = pltpu.SemaphoreType.DMA
        nears, fars = rows // NEAR_ROWS, len(FAR_CHUNKS)
        scalar = pltpu.SMEM((1,), jnp.float32)
        last = pltpu.VMEM((LAST_ROWS, depth), jnp.bfloat16)
        last_weights = pltpu.VMEM((rows, LAST_ROWS), jnp.bfloat16)
        in_vmem = pl.BlockSpec(memory_space=pltpu.VMEM)
        in_hbm = pl.BlockSpec(memory_space=pltpu.HBM)
        operands = [
            pltpu.with_memory_space_constraint(operand, pltpu.HBM)
            for operand in (images, texts)
        ]
        parts = pl.pallas_call(
            functools.partial(kernel, n),
            out_shape=(block, total, block, inverses, last, last_weights),
            in_specs=[in_hbm] * 2 + [pl.BlockSpec(memory_space=pl.ANY)] * 2,
            out_specs=[in_vmem] * 6,
            scratch_shapes=[scalar] * 2
            + [block] * 5
            + [block] * 3
            + [inverses]
            + [total]
            + [
                dma((4,)),
                dma((1,)),
                dma((1,)),
                dma((nears,)),
                dma((nears,)),
                dma((nears,)),
                dma((nears,)),
                dma((fars,)),
                dma((fars,)),
                pltpu.VMEM((len(DETOUR) * DETOUR_ROWS, depth), jnp.bfloat16),
                dma((len(DETOUR),)),
                dma((len(DETOUR),)),
                pltpu.SemaphoreType.REGULAR,
                pltpu.SemaphoreType.REGULAR,
            ],
            compiler_params=pltpu.CompilerParams(
                collective_id=0, has_side_effects=True, vmem_limit_bytes=40 * 1024 * 1024
            ),
            cost_estimate=pl.CostEstimate(
                flops=24 * rows * rows * depth, bytes_accessed=8 * rows * depth, transcendentals=0
            ),
        )(*operands, logit_scale, logit_bias)
        parts = [pltpu.with_memory_space_constraint(part, pltpu.VMEM) for part in parts]
        result = jax.ShapeDtypeStruct((rows, depth), jnp.bfloat16)
        return pl.pallas_call(
            finish_kernel,
            out_shape=(result, result),
            in_specs=[in_vmem] * 6,
            out_specs=[in_hbm] * 2,
            scratch_shapes=[block, dma, dma((rows // STORE_ROWS,))],
            compiler_params=pltpu.CompilerParams(vmem_limit_bytes=16 * 1024 * 1024),
            cost_estimate=pl.CostEstimate(
                flops=8 * rows * depth, bytes_accessed=4 * rows * depth, transcendentals=0
            ),
        )(*parts)

    in_specs = (P("dp", None), P("dp", None), P(), P())
    out_specs = (P("dp", None), P("dp", None))
    return jax.shard_map(shards, mesh=mesh, in_specs=in_specs, out_specs=out_specs, check_vma=False)
```
